256 devices in a mesh: gx: 8 (over z), gy: 8 (over y_hi, x), col: 4 (over y_lo, core).
Axes of the slice: x: 4, y: 4 (y_hi: 2, y_lo: 2; y = y_hi * 2 + y_lo), z: 8, core: 2. Of those that a mesh axis runs over, the one named last changes fastest.
Arguments:
- volume: bfloat16 [1, 128, 64, 64, 128], P(None, 'col', 'gx', 'gy'), may hold values from -6 to 6
- weight_one: bfloat16 [3, 3, 3, 128, 128], P(None, None, None, 'col'), may hold values from -0.109375 to 0.109375
- bias_one: float32 [128], P('col'), may hold values from -3 to 3
- weight_two: bfloat16 [3, 3, 3, 128, 128], P(None, None, None, 'col'), may hold values from -0.109375 to 0.109375
- bias_two: float32 [128], P('col'), may hold values from -3 to 3
Outputs:
- activations: bfloat16 [1, 128, 64, 64, 128], P(None, 'col', 'gx', 'gy')
The draws below stay inside these ranges and needn't reach their ends.
All inputs are finite; a program needn't handle non-finite values.
Results may differ from the reference program's by a relative error of at most 0.01.
Values may be sent and summed in bfloat16 or wider, within the bound.
A program may use at most 64 MiB of HBM per device.

```python
import jax
import jax.numpy as jnp
from jax import lax

C = 128
NZ = 128
BATCH = 1
NX = 64
NY = 64


def level_of(rng, dims, pieces, low, top_value):
    loudness = 1.0
    for axis_at, blocks in pieces:
        steps = jax.random.uniform(jax.random.fold_in(jax.random.fold_in(rng, 6), axis_at), (blocks,), jnp.float32, low / len(pieces), top_value / len(pieces))
        loudness = loudness * jnp.repeat(jnp.exp(steps), dims[axis_at] // blocks).reshape((-1,) + (1,) * (len(dims) - 1 - axis_at))
    return loudness


def centred(rng, dims, scale, reach, split=(), kind=jnp.bfloat16):
    level = level_of(rng, dims, split, -0.22, 0.18) if split else 1.0
    result = jax.random.normal(rng, dims, jnp.float32) * scale * level
    return jnp.minimum(jnp.maximum(result, -reach), reach).astype(kind)


def setup_inputs(seed: int = 0) -> dict:
    streams_of = jax.random.split(jax.random.key(seed), 6)
    return {
        "volume": centred(streams_of[0], (BATCH, C, NX, NY, NZ), 1.0, 6.0, ((1, 4), (2, 8), (3, 8))),
        "weight_one": centred(streams_of[1], (3, 3, 3, C, C), (27 * C) ** -0.5, 0.109375, ((3, 4),)),
        "bias_one": centred(streams_of[2], (C,), 0.5, 3.0, ((0, 4),), jnp.float32),
        "weight_two": centred(streams_of[3], (3, 3, 3, C, C), (27 * C) ** -0.5, 0.109375, ((3, 4),)),
        "bias_two": centred(streams_of[4], (C,), 0.5, 3.0, ((0, 4),), jnp.float32),
    }


def conv_layer(volume, weight, layer_bias):
    padded = jnp.pad(volume.astype(jnp.float32), ((0, 0), (0, 0), (1, 1), (1, 1), (1, 1)), mode="wrap")
    total = lax.conv_general_dilated(padded, weight.astype(jnp.float32), (1, 1, 1), "VALID", dimension_numbers=("NCDHW", "DHWOI", "NCDHW"), precision=lax.Precision.HIGHEST)
    return jax.nn.relu(total + layer_bias[None, :, None, None, None]).astype(jnp.bfloat16)


def reference(volume, weight_one, bias_one, weight_two, bias_two):
    hidden = conv_layer(volume, weight_one, bias_one)
    return conv_layer(hidden, weight_two, bias_two)
```

```python
import jax
import jax.numpy as jnp
from jax import lax
from jax.experimental import pallas as pl
from jax.experimental.pallas import tpu as pltpu
from jax.sharding import PartitionSpec as P

BF16 = jnp.bfloat16
F32 = jnp.float32
MESH = pl.DeviceIdType.MESH
MATES = ((1, 0), (0, 1), (1, 1))
AROUND = ((-1, 0), (1, 0), (0, -1), (0, 1), (-1, -1), (-1, 1), (1, -1), (1, 1))
TAPS = tuple((dx, dy) for dx in range(3) for dy in range(3))


def mo(value, unit):
    return pl.multiple_of(value, unit)


def kernel(
    vol, w1, w2, b1, b2, out,
    part, cells, hidden, weights, bias_part, bias, result, final,
    local_sem, mate_s, mate_r, ext_s, ext_r, w_s, w_r, b_s, b_r, h_s, h_r, o_s, o_r,
):
    gx, gy, col = lax.axis_index("gx"), lax.axis_index("gy"), lax.axis_index("col")
    a, k = col // 2, col % 2
    xs, ys = (a + gx) % 2, (k + gy) % 2
    big_x, big_y = 2 * gx + xs, 2 * gy + ys
    mine = mo(32 * col, 32)

    def at(to_x, to_y):
        to_x, to_y = (to_x + 16) % 16, (to_y + 16) % 16
        tx, ty = to_x // 2, to_y // 2
        return tx, ty, 2 * ((to_x % 2 + tx) % 2) + (to_y % 2 + ty) % 2

    around = [at(big_x + dx, big_y + dy) for dx, dy in AROUND]
    mates = [(gx, gy, 2 * ((a + fx) % 2) + (k + fy) % 2) for fx, fy in MATES]
    across = [(gx, (gy + 4) % 8, 2 * (1 - a) + (k + d) % 2) for d in range(2)]
    w_to = [mates[1]] + across

    barrier = pltpu.get_barrier_semaphore()
    for device in around + across:
        pl.semaphore_signal(barrier, inc=1, device_id=device, device_id_type=MESH)

    def remote(src, dst, s, r, device):
        return pltpu.make_async_remote_copy(
            src_ref=src, dst_ref=dst, send_sem=s, recv_sem=r, device_id=device, device_id_type=MESH
        )

    own_w = [
        pltpu.make_async_copy(w, weights.at[l, :, pl.ds(mine, 32), :], local_sem.at[l])
        for l, w in enumerate((w1, w2))
    ]
    for c in own_w:
        c.start()

    for x in range(8):
        rows = jnp.swapaxes(vol[:, x], 0, 1)
        for y in range(8):
            part[x, :, y * 128 : (y + 1) * 128] = rows[y]
    eye = lax.broadcasted_iota(jnp.int32, (32, 32), 0) == lax.broadcasted_iota(jnp.int32, (32, 32), 1)
    for l, b in enumerate((b1, b2)):
        column = jnp.sum(jnp.where(eye, b[...], 0.0), axis=1, keepdims=True)
        bias_part[:, l * 64 : (l + 1) * 64] = jnp.broadcast_to(column, (32, 64))

    pl.semaphore_wait(barrier, len(around) + len(across))

    def block(xq, yq):
        return part.at[pl.ds(3 * xq, 5), :, pl.ds(mo(384 * yq, 128), 640)]

    def place(xq, yq):
        return cells.at[pl.ds(1 - xq, 5), pl.ds(mine, 32), pl.ds(mo(128 * (1 - yq), 128), 640)]

    mate_copies = []
    for i, (fx, fy) in enumerate(MATES):
        xq, yq = (xs + fx) % 2, (ys + fy) % 2
        c = remote(block(xq, yq), place(xq, yq), mate_s.at[i], mate_r.at[i], mates[i])
        c.start()
        mate_copies.append(c)
    own_cells = pltpu.make_async_copy(block(xs, ys), place(xs, ys), local_sem.at[2])
    own_cells.start()
    own_bias = pltpu.make_async_copy(bias_part, bias.at[pl.ds(mine, 32), :], local_sem.at[3])
    own_bias.start()
    w_copies = [[], []]
    b_copies = []
    for i in range(3):
        c = remote(bias_part, bias.at[pl.ds(mine, 32), :], b_s.at[i], b_r.at[i], mates[i])
        c.start()
        b_copies.append(c)
    for l, w in enumerate((w1, w2)):
        for i in range(3):
            c = remote(w, weights.at[l, :, pl.ds(mine, 32), :], w_s.at[l, i], w_r.at[l, i], w_to[i])
            c.start()
            w_copies[l].append(c)

    own_cells.wait()
    for c in mate_copies:
        c.wait_recv()

    row, col_at = 1 + 3 * xs, mo(128 * (1 + 3 * ys), 128)
    row_to, col_to = 5 * (1 - xs), mo(640 * (1 - ys), 128)
    rows5, lanes5 = pl.ds(1 - xs, 5), pl.ds(mo(128 * (1 - ys), 128), 640)
    ext = [
        remote(
            cells.at[pl.ds(row, 1), :, lanes5], cells.at[pl.ds(row_to, 1), :, lanes5],
            ext_s.at[0], ext_r.at[0], at(big_x + 2 * xs - 1, big_y),
        ),
        remote(
            cells.at[rows5, :, pl.ds(col_at, 128)], cells.at[rows5, :, pl.ds(col_to, 128)],
            ext_s.at[1], ext_r.at[1], at(big_x, big_y + 2 * ys - 1),
        ),
        remote(
            cells.at[pl.ds(row, 1), :, pl.ds(col_at, 128)], cells.at[pl.ds(row_to, 1), :, pl.ds(col_to, 128)],
            ext_s.at[2], ext_r.at[2], at(big_x + 2 * xs - 1, big_y + 2 * ys - 1),
        ),
    ]
    for c in ext:
        c.start()

    own_bias.wait()
    for c in b_copies:
        c.wait_recv()
    own_w[0].wait()
    for c in w_copies[0]:
        c.wait_recv()
    for c in ext:
        c.wait_recv()

    def conv(source, l, x):
        stacked = jnp.concatenate(
            [
                jnp.concatenate([weights[l, (dx * 3 + dy) * 3 + dz] for dx, dy in TAPS], axis=1)
                for dz in range(3)
            ],
            axis=0,
        )
        shift = bias[:, l * 64 : l * 64 + 1]
        pieces = []
        for y in (0, 2):
            right = jnp.concatenate(
                [source[x + dx, :, (y + dy) * 128 : (y + dy + 2) * 128] for dx, dy in TAPS], axis=0
            )
            terms = jnp.dot(stacked, right, preferred_element_type=F32)
            for j in range(2):
                t = terms[:, j * 128 : (j + 1) * 128]
                total = pltpu.roll(t[0:128], 1, axis=1) + t[128:256] + pltpu.roll(t[256:384], 127, axis=1)
                pieces.append(jnp.maximum(total + shift, 0.0).astype(BF16))
        return pieces

    def first(x):
        for y, piece in enumerate(conv(cells, 0, x)):
            hidden[x + 1, :, (y + 1) * 128 : (y + 2) * 128] = piece

    def halo(i):
        dx, dy = AROUND[i]
        spans = {-1: (1, 5), 1: (4, 0)}
        fx, tx = spans.get(dx, (1, 1))
        fy, ty = spans.get(dy, (1, 1))
        nx, ny = (1 if dx else 4), (128 if dy else 512)
        return remote(
            hidden.at[pl.ds(fx, nx), :, pl.ds(fy * 128, ny)],
            hidden.at[pl.ds(tx, nx), :, pl.ds(ty * 128, ny)],
            h_s.at[i], h_r.at[i], around[i],
        )

    halos = [halo(i) for i in range(8)]

    @pl.loop(0, 2)
    def _(i):
        first(3 * i)

    for i in (0, 1, 4, 5, 6, 7):
        halos[i].start()

    @pl.loop(1, 3)
    def _(i):
        first(i)

    for i in (2, 3):
        halos[i].start()

    own_w[1].wait()
    for c in w_copies[1]:
        c.wait_recv()
    for c in halos:
        c.wait_recv()

    def spread(x, i):
        other = 2 * ((a + MATES[i][0]) % 2) + (k + MATES[i][1]) % 2
        return remote(
            result.at[pl.ds(x, 1), pl.ds(mo(32 * other, 32), 32), :],
            final.at[pl.ds(4 * xs + x, 1), :, pl.ds(mo(512 * ys, 512), 512)],
            o_s.at[i, x], o_r.at[i, x], mates[i],
        )

    def own_result():
        return pltpu.make_async_copy(
            result.at[:, pl.ds(mine, 32), :],
            final.at[pl.ds(4 * xs, 4), :, pl.ds(mo(512 * ys, 512), 512)],
            local_sem.at[4],
        )

    @pl.loop(0, 4)
    def _(x):
        for y, piece in enumerate(conv(hidden, 1, x)):
            result[x, :, y * 128 : (y + 1) * 128] = piece
        for i in range(3):
            spread(x, i).start()

    own_result().start()
    own_result().wait()
    for x in range(4):
        for i in range(3):
            spread(x, i).wait_recv()

    for x in range(8):
        rows = jnp.stack([final[x, :, y * 128 : (y + 1) * 128] for y in range(8)], axis=0)
        out[:, x] = jnp.swapaxes(rows, 0, 1)

    for c in mate_copies + b_copies + w_copies[0] + w_copies[1] + ext + halos:
        c.wait_send()
    for x in range(4):
        for i in range(3):
            spread(x, i).wait_send()


def local(volume, weight_one, bias_one, weight_two, bias_two):
    vmem = pl.BlockSpec(memory_space=pltpu.VMEM)
    hbm = pl.BlockSpec(memory_space=pl.ANY)
    dma = pltpu.SemaphoreType.DMA
    out = pl.pallas_call(
        kernel,
        out_shape=jax.ShapeDtypeStruct((32, 8, 8, 128), BF16),
        in_specs=[vmem, hbm, hbm, vmem, vmem],
        out_specs=vmem,
        scratch_shapes=[
            pltpu.VMEM((8, 32, 1024), BF16),
            pltpu.VMEM((6, 128, 768), BF16),
            pltpu.VMEM((6, 128, 768), BF16),
            pltpu.VMEM((2, 27, 128, 128), BF16),
            pltpu.VMEM((32, 128), F32),
            pltpu.VMEM((128, 128), F32),
            pltpu.VMEM((4, 128, 512), BF16),
            pltpu.VMEM((8, 32, 1024), BF16),
            dma((5,)),
            dma((3,)), dma((3,)),
            dma((3,)), dma((3,)),
            dma((2, 3)), dma((2, 3)),
            dma((3,)), dma((3,)),
            dma((8,)), dma((8,)),
            dma((3, 4)), dma((3, 4)),
        ],
        compiler_params=pltpu.CompilerParams(
            collective_id=0, has_side_effects=True, vmem_limit_bytes=48 * 2**20
        ),
        cost_estimate=pl.CostEstimate(flops=3_700_000_000, bytes_accessed=3_000_000, transcendentals=0),
    )(
        volume.reshape(32, 8, 8, 128),
        weight_one.reshape(27, 32, 128),
        weight_two.reshape(27, 32, 128),
        bias_one.reshape(1, 32),
        bias_two.reshape(1, 32),
    )
    return out.reshape(1, 32, 8, 8, 128)


def solution(mesh):
    in_specs = (
        P(None, "col", "gx", "gy", None),
        P(None, None, None, "col", None),
        P("col"),
        P(None, None, None, "col", None),
        P("col"),
    )
    out_specs = P(None, "col", "gx", "gy", None)
    return jax.shard_map(local, mesh=mesh, in_specs=in_specs, out_specs=out_specs, check_vma=False)
```

```python
import jax
import jax.numpy as jnp
from jax import lax
from jax.experimental import pallas as pl
from jax.experimental.pallas import tpu as pltpu
from jax.sharding import PartitionSpec as P

BF16 = jnp.bfloat16
F32 = jnp.float32
MESH = pl.DeviceIdType.MESH
MATES = ((1, 0), (1, 1), (0, 1))
AROUND = ((-1, 0), (1, 0), (0, -1), (0, 1), (-1, -1), (-1, 1), (1, -1), (1, 1))
TAPS = tuple((dx, dy) for dx in range(3) for dy in range(3))


def mo(value, unit):
    return pl.multiple_of(value, unit)


def kernel(
    vol_in, w1, w2, b1_in, b2_in, out,
    vol, b1, b2, part, cells, hidden, weights, bias_part, bias, result, final,
    in_sem, own_sem, mate_s, mate_r, ext_s, ext_r, w_s, w_r, b_s, b_r, h_s, h_r, o_s, o_r,
):
    gx, gy, col = lax.axis_index("gx"), lax.axis_index("gy"), lax.axis_index("col")
    a, k = col // 2, col % 2
    xs, ys = (a + gx) % 2, (k + gy) % 2
    big_x, big_y = 2 * gx + xs, 2 * gy + ys
    mine = mo(32 * col, 32)

    def at(to_x, to_y):
        to_x, to_y = (to_x + 16) % 16, (to_y + 16) % 16
        tx, ty = to_x // 2, to_y // 2
        return tx, ty, 2 * ((to_x % 2 + tx) % 2) + (to_y % 2 + ty) % 2

    around = [at(big_x + dx, big_y + dy) for dx, dy in AROUND]
    mates = [(gx, gy, 2 * ((a + fx) % 2) + (k + fy) % 2) for fx, fy in MATES]
    sibling = mates[2]
    across = (gx, (gy + 4) % 8, 2 * (1 - a) + k)

    barrier = pltpu.get_barrier_semaphore()
    for device in around + [across]:
        pl.semaphore_signal(barrier, inc=1, device_id=device, device_id_type=MESH)

    def remote(src, dst, s, r, device):
        return pltpu.make_async_remote_copy(
            src_ref=src, dst_ref=dst, send_sem=s, recv_sem=r, device_id=device, device_id_type=MESH
        )

    fetch = [
        pltpu.make_async_copy(src, dst, in_sem.at[i])
        for i, (src, dst) in enumerate(((vol_in, vol), (b1_in, b1), (b2_in, b2)))
    ]
    own_w = [
        pltpu.make_async_copy(w, weights.at[l, :, pl.ds(mine, 32), :], in_sem.at[3 + l])
        for l, w in enumerate((w1, w2))
    ]
    for c in fetch + own_w:
        c.start()
    for c in fetch:
        c.wait()

    for x in range(8):
        rows = jnp.swapaxes(vol[:, x], 0, 1)
        for y in range(8):
            part[x, :, y * 128 : (y + 1) * 128] = rows[y]
    eye = lax.broadcasted_iota(jnp.int32, (32, 32), 0) == lax.broadcasted_iota(jnp.int32, (32, 32), 1)
    for l, b in enumerate((b1, b2)):
        column = jnp.sum(jnp.where(eye, b[...], 0.0), axis=1, keepdims=True)
        bias_part[:, l * 64 : (l + 1) * 64] = jnp.broadcast_to(column, (32, 64))

    pl.semaphore_wait(barrier, len(around) + 1)

    def piece(x0, nx, y0, ny, to_x, to_y):
        return (
            part.at[pl.ds(x0, nx), :, pl.ds(mo(128 * y0, 128), 128 * ny)],
            cells.at[pl.ds(to_x, nx), pl.ds(mine, 32), pl.ds(128 * to_y, 128 * ny)],
        )

    early, late = [], []
    for i in range(2):
        xq, yq = (xs + MATES[i][0]) % 2, (ys + MATES[i][1]) % 2
        pieces = (
            piece(7 * xq, 1, 4 * yq, 4, 1 + 3 * xq, 1),
            piece(1 + 2 * xq, 4, 4 * yq, 1, 2 - 2 * xq, 1),
            piece(1 + 2 * xq, 4, 4 * yq + 3, 1, 2 - 2 * xq, 4),
            piece(1 + 2 * xq, 4, 4 * yq + 1, 2, 2 - 2 * xq, 2),
        )
        copies = [remote(s, d, mate_s.at[i, j], mate_r.at[i, j], mates[i]) for j, (s, d) in enumerate(pieces)]
        early.extend(copies[:3])
        late.append(copies[3])
    src, dst = piece(3 * xs, 5, 4 * ((ys + 1) % 2), 4, 1 - xs, 1)
    near = remote(src, dst, mate_s.at[2, 0], mate_r.at[2, 0], sibling)
    src, dst = piece(3 * xs, 5, 4 * ys, 4, 1 - xs, 1)
    own_cells = pltpu.make_async_copy(src, dst, own_sem.at[0])
    own_bias = pltpu.make_async_copy(bias_part, bias.at[pl.ds(mine, 32), :], own_sem.at[1])
    w_far, w_near, w_on = [], [], []
    theirs = mo(64 * (1 - a) + 32 * k, 32)
    for l, w in enumerate((w1, w2)):
        slot, other = weights.at[l, :, pl.ds(mine, 32), :], weights.at[l, :, pl.ds(theirs, 32), :]
        w_far.append(remote(w, slot, w_s.at[l, 0], w_r.at[l, 0], across))
        w_near.append(remote(w, slot, w_s.at[l, 1], w_r.at[l, 1], sibling))
        w_on.append(remote(other, other, w_s.at[l, 2], w_r.at[l, 2], sibling))
    b_copies = [
        remote(bias_part, bias.at[pl.ds(mine, 32), :], b_s.at[i], b_r.at[i], mates[i]) for i in range(3)
    ]

    own_cells.start()
    near.start()
    for c in early:
        c.start()
    w_far[0].start()
    w_near[0].start()
    own_bias.start()
    for c in late:
        c.start()
    for c in b_copies:
        c.start()

    row, row_to = 1 + 3 * xs, 5 * (1 - xs)
    rows5 = pl.ds(1 - xs, 5)
    x_out = big_x + 2 * xs - 1

    def edges(j):
        half = pl.ds(mo(64 * (a if j == 0 else 1 - a), 64), 64)
        spots = (
            (pl.ds(row, 1), pl.ds(row_to, 1), 128, 128, 512, at(x_out, big_y)),
            (rows5, rows5, 512, 0, 128, at(big_x, big_y + 1)),
            (rows5, rows5, 128, 640, 128, at(big_x, big_y - 1)),
            (pl.ds(row, 1), pl.ds(row_to, 1), 512, 0, 128, at(x_out, big_y + 1)),
            (pl.ds(row, 1), pl.ds(row_to, 1), 128, 640, 128, at(x_out, big_y - 1)),
        )
        return [
            remote(
                cells.at[rf, half, pl.ds(lf, n)], cells.at[rt, half, pl.ds(lt, n)],
                ext_s.at[j, i], ext_r.at[j, i], device,
            )
            for i, (rf, rt, lf, lt, n, device) in enumerate(spots)
        ]

    ext = [edges(0), edges(1)]
    own_cells.wait()
    near.wait_recv()
    for c in ext[0]:
        c.start()
    for c in early:
        c.wait_recv()
    for c in ext[1]:
        c.start()
    w_far[0].wait_recv()
    w_on[0].start()
    w_far[1].start()
    w_near[1].start()
    own_bias.wait()
    for c in own_w:
        c.wait()
    for c in b_copies + late + [w_near[0]] + ext[0] + ext[1] + [w_on[0]]:
        c.wait_recv()

    def conv(source, l, x):
        stacked = jnp.concatenate(
            [
                jnp.concatenate([weights[l, (dx * 3 + dy) * 3 + dz] for dx, dy in TAPS], axis=1)
                for dz in range(3)
            ],
            axis=0,
        )
        shift = bias[:, l * 64 : l * 64 + 1]
        pieces = []
        for y in (0, 2):
            right = jnp.concatenate(
                [source[x + dx, :, (y + dy) * 128 : (y + dy + 2) * 128] for dx, dy in TAPS], axis=0
            )
            terms = jnp.dot(stacked, right, preferred_element_type=F32)
            for j in range(2):
                t = terms[:, j * 128 : (j + 1) * 128]
                total = pltpu.roll(t[0:128], 1, axis=1) + t[128:256] + pltpu.roll(t[256:384], 127, axis=1)
                pieces.append(jnp.maximum(total + shift, 0.0).astype(BF16))
        return pieces

    def first(x):
        for y, value in enumerate(conv(cells, 0, x)):
            hidden[x + 1, :, (y + 1) * 128 : (y + 2) * 128] = value

    def halo(i, from_x, nx, from_y, ny, to_x, to_y, device):
        return remote(
            hidden.at[pl.ds(from_x, nx), :, pl.ds(from_y * 128, ny * 128)],
            hidden.at[pl.ds(to_x, nx), :, pl.ds(to_y * 128, ny * 128)],
            h_s.at[i], h_r.at[i], device,
        )

    x_low, x_high, y_low, y_high, ll, lh, hl, hh = around
    outer = [
        halo(0, 1, 1, 1, 4, 5, 1, x_low),
        halo(1, 4, 1, 1, 4, 0, 1, x_high),
        halo(2, 1, 1, 1, 1, 5, 5, ll),
        halo(3, 1, 1, 4, 1, 5, 0, lh),
        halo(4, 4, 1, 1, 1, 0, 5, hl),
        halo(5, 4, 1, 4, 1, 0, 0, hh),
    ]
    sides = [
        [
            halo(6 + 2 * j, x, n, 1, 1, x, 5, y_low),
            halo(7 + 2 * j, x, n, 4, 1, x, 0, y_high),
        ]
        for j, (x, n) in enumerate(((1, 1), (4, 1), (2, 2)))
    ]

    @pl.loop(0, 2)
    def _(i):
        first(3 * i)

    for c in outer[:2] + sides[0] + sides[1] + outer[2:]:
        c.start()

    @pl.loop(1, 3)
    def _(i):
        first(i)

    for c in sides[2]:
        c.start()
    w_far[1].wait_recv()
    w_on[1].start()
    for pair in sides:
        for c in pair:
            c.wait_recv()
    w_near[1].wait_recv()
    w_on[1].wait_recv()

    def spread(x, i):
        other = 2 * ((a + MATES[i][0]) % 2) + (k + MATES[i][1]) % 2
        return remote(
            result.at[pl.ds(x, 1), pl.ds(mo(32 * other, 32), 32), :],
            final.at[pl.ds(4 * xs + x, 1), :, pl.ds(mo(512 * ys, 512), 512)],
            o_s.at[i, x], o_r.at[i, x], mates[i],
        )

    def own_result(x):
        return pltpu.make_async_copy(
            result.at[pl.ds(x, 1), pl.ds(mine, 32), :],
            final.at[pl.ds(4 * xs + x, 1), :, pl.ds(mo(512 * ys, 512), 512)],
            own_sem.at[2 + x],
        )

    def second(x):
        for y, value in enumerate(conv(hidden, 1, x)):
            result[x, :, y * 128 : (y + 1) * 128] = value
        for i in range(3):
            spread(x, i).start()
        own_result(x).start()

    @pl.loop(1, 3)
    def _(x):
        second(x)

    for c in outer:
        c.wait_recv()

    @pl.loop(0, 2)
    def _(x):
        second(3 * x)

    for x in (1, 2, 0, 3):
        own_result(x).wait()
        for i in range(3):
            spread(x, i).wait_recv()
        for at_x in (x, x + 4):
            rows = jnp.stack([final[at_x, :, y * 128 : (y + 1) * 128] for y in range(8)], axis=0)
            out[:, at_x] = jnp.swapaxes(rows, 0, 1)

    for c in early + late + [near] + b_copies + w_far + w_near + w_on + ext[0] + ext[1] + outer:
        c.wait_send()
    for pair in sides:
        for c in pair:
            c.wait_send()
    for x in range(4):
        for i in range(3):
            spread(x, i).wait_send()


def local(volume, weight_one, bias_one, weight_two, bias_two):
    vmem = pl.BlockSpec(memory_space=pltpu.VMEM)
    hbm = pl.BlockSpec(memory_space=pl.ANY)
    dma = pltpu.SemaphoreType.DMA
    out = pl.pallas_call(
        kernel,
        out_shape=jax.ShapeDtypeStruct((32, 8, 8, 128), BF16),
        in_specs=[hbm] * 5,
        out_specs=vmem,
        scratch_shapes=[
            pltpu.VMEM((32, 8, 8, 128), BF16),
            pltpu.VMEM((1, 32), F32),
            pltpu.VMEM((1, 32), F32),
            pltpu.VMEM((8, 32, 1024), BF16),
            pltpu.VMEM((6, 128, 768), BF16),
            pltpu.VMEM((6, 128, 768), BF16),
            pltpu.VMEM((2, 27, 128, 128), BF16),
            pltpu.VMEM((32, 128), F32),
            pltpu.VMEM((128, 128), F32),
            pltpu.VMEM((4, 128, 512), BF16),
            pltpu.VMEM((8, 32, 1024), BF16),
            dma((5,)), dma((6,)),
            dma((3, 4)), dma((3, 4)),
            dma((2, 5)), dma((2, 5)),
            dma((2, 3)), dma((2, 3)),
            dma((3,)), dma((3,)),
            dma((12,)), dma((12,)),
            dma((3, 4)), dma((3, 4)),
        ],
        compiler_params=pltpu.CompilerParams(
            collective_id=0, has_side_effects=True, vmem_limit_bytes=60 * 2**20
        ),
        cost_estimate=pl.CostEstimate(flops=3_700_000_000, bytes_accessed=3_000_000, transcendentals=0),
    )(
        volume.reshape(32, 8, 8, 128),
        weight_one.reshape(27, 32, 128),
        weight_two.reshape(27, 32, 128),
        bias_one.reshape(1, 32),
        bias_two.reshape(1, 32),
    )
    return out.reshape(1, 32, 8, 8, 128)


def solution(mesh):
    in_specs = (
        P(None, "col", "gx", "gy", None),
        P(None, None, None, "col", None),
        P("col"),
        P(None, None, None, "col", None),
        P("col"),
    )
    out_specs = P(None, "col", "gx", "gy", None)
    return jax.shard_map(local, mesh=mesh, in_specs=in_specs, out_specs=out_specs, check_vma=False)
```

```python
import jax
import jax.numpy as jnp
from jax import lax
from jax.experimental import pallas as pl
from jax.experimental.pallas import tpu as pltpu
from jax.sharding import PartitionSpec as P

BF16 = jnp.bfloat16
F32 = jnp.float32
MESH = pl.DeviceIdType.MESH
MATES = ((1, 0), (1, 1), (0, 1))


def mo(value, unit):
    return pl.multiple_of(value, unit)


def kernel(
    vol_in, w1, w2, b1_in, b2_in, out,
    vol, b1, b2, part, cells, hidden, weights, bias_part, bias, result, final,
    in_sem, own_sem, mate_s, mate_r, ext_s, ext_r, w_s, w_r, b_s, b_r, h_s, h_r, o_s, o_r,
):
    gx, gy, col = lax.axis_index("gx"), lax.axis_index("gy"), lax.axis_index("col")
    a, k = col // 2, col % 2
    xs, ys = (a + gx + gy // 4) % 2, (k + gy) % 2
    big_x, big_y = 2 * gx + xs, 2 * gy + ys
    mine = mo(32 * col, 32)

    def at(to_x, to_y):
        to_x, to_y = (to_x + 16) % 16, (to_y + 16) % 16
        tx, ty = to_x // 2, to_y // 2
        return tx, ty, 2 * ((to_x % 2 + tx + ty // 4) % 2) + (to_y % 2 + ty) % 2

    mates = [(gx, gy, 2 * ((a + fx) % 2) + (k + fy) % 2) for fx, fy in MATES]
    sibling = mates[2]
    across = (gx, (gy + 4) % 8, 2 * (1 - a) + k)
    x_next = at(big_x + 2 * xs - 1, big_y)
    y_next = at(big_x, big_y + 2 * ys - 1)
    y_pair = at(big_x, big_y + 1), at(big_x, big_y - 1)
    next_pair = at(big_x + 2 * xs - 1, big_y + 1), at(big_x + 2 * xs - 1, big_y - 1)
    mate_pair = at(big_x + 1 - 2 * xs, big_y + 1), at(big_x + 1 - 2 * xs, big_y - 1)
    far_corner = at(big_x + 1 - 2 * xs, big_y + 2 * ys - 1)

    barrier = pltpu.get_barrier_semaphore()
    partners = mates + [across, x_next, y_next, far_corner, next_pair[0], next_pair[1]]
    for device in partners:
        pl.semaphore_signal(barrier, inc=1, device_id=device, device_id_type=MESH)

    def remote(src, dst, s, r, device):
        return pltpu.make_async_remote_copy(
            src_ref=src, dst_ref=dst, send_sem=s, recv_sem=r, device_id=device, device_id_type=MESH
        )

    fetch = [
        pltpu.make_async_copy(src, dst, in_sem.at[i])
        for i, (src, dst) in enumerate(((vol_in, vol), (b1_in, b1), (b2_in, b2)))
    ]
    own_w = [
        pltpu.make_async_copy(w, weights.at[l, :, pl.ds(mine, 32), :], in_sem.at[3 + l])
        for l, w in enumerate((w1, w2))
    ]
    for c in fetch + own_w:
        c.start()
    for c in fetch:
        c.wait()

    for x in range(8):
        rows = jnp.swapaxes(vol[:, x], 0, 1)
        for y in range(8):
            part[x, :, y * 128 : (y + 1) * 128] = rows[y]
    eye = lax.broadcasted_iota(jnp.int32, (32, 32), 0) == lax.broadcasted_iota(jnp.int32, (32, 32), 1)
    for l, b in enumerate((b1, b2)):
        column = jnp.sum(jnp.where(eye, b[...], 0.0), axis=1, keepdims=True)
        bias_part[:, l * 64 : (l + 1) * 64] = jnp.broadcast_to(column, (32, 64))

    pl.semaphore_wait(barrier, len(partners))

    def piece(x0, nx, y0, ny, to_x, to_y):
        return (
            part.at[pl.ds(x0, nx), :, pl.ds(mo(128 * y0, 128), 128 * ny)],
            cells.at[pl.ds(to_x, nx), pl.ds(mine, 32), pl.ds(128 * to_y, 128 * ny)],
        )

    early, late = [], []
    for i in range(2):
        xq, yq = (xs + MATES[i][0]) % 2, (ys + MATES[i][1]) % 2
        pieces = (
            piece(7 * xq, 1, 4 * yq, 4, 1 + 3 * xq, 1),
            piece(1 + 2 * xq, 4, 4 * yq, 1, 2 - 2 * xq, 1),
            piece(1 + 2 * xq, 4, 4 * yq + 3, 1, 2 - 2 * xq, 4),
            piece(1 + 2 * xq, 4, 4 * yq + 1, 2, 2 - 2 * xq, 2),
        )
        copies = [remote(s, d, mate_s.at[i, j], mate_r.at[i, j], mates[i]) for j, (s, d) in enumerate(pieces)]
        early.extend(copies[:3])
        late.append(copies[3])
    src, dst = piece(3 * xs, 5, 4 * ((ys + 1) % 2), 4, 1 - xs, 1)
    near = remote(src, dst, mate_s.at[2, 0], mate_r.at[2, 0], sibling)
    src, dst = piece(3 * xs, 5, 4 * ys, 4, 1 - xs, 1)
    own_cells = pltpu.make_async_copy(src, dst, own_sem.at[0])
    own_bias = pltpu.make_async_copy(bias_part, bias.at[pl.ds(mine, 32), :], own_sem.at[1])
    theirs = mo(64 * (1 - a) + 32 * k, 32)

    def send_w(l, w, first_tap, n_taps, i, device):
        slot = weights.at[l, pl.ds(first_tap, n_taps), pl.ds(mine, 32), :]
        return remote(w.at[pl.ds(first_tap, n_taps)], slot, w_s.at[i], w_r.at[i], device)

    def pass_w(l, i):
        slot = weights.at[l, :, pl.ds(theirs, 32), :]
        return remote(slot, slot, w_s.at[i], w_r.at[i], sibling)

    w1_far, w1_near, w1_on = send_w(0, w1, 0, 27, 0, across), send_w(0, w1, 0, 27, 1, sibling), pass_w(0, 2)
    w2_far = [send_w(1, w2, 0, 14, 3, mates[0]), send_w(1, w2, 14, 13, 4, across)]
    w2_near, w2_on = send_w(1, w2, 0, 27, 5, sibling), pass_w(1, 6)
    b_copies = [
        remote(bias_part, bias.at[pl.ds(mine, 32), :], b_s.at[i], b_r.at[i], mates[i]) for i in range(3)
    ]

    own_cells.start()
    near.start()
    for c in early:
        c.start()
    w1_far.start()
    w1_near.start()
    own_bias.start()
    for c in late:
        c.start()
    for c in b_copies:
        c.start()

    end, end_to = 1 + 3 * xs, 5 * (1 - xs)
    rows5 = pl.ds(1 - xs, 5)

    def edges(j):
        half = pl.ds(mo(64 * (a if j == 0 else 1 - a), 64), 64)
        spots = (
            (pl.ds(end, 1), pl.ds(end_to, 1), 128, 128, 512, x_next),
            (rows5, rows5, 512, 0, 128, y_pair[0]),
            (rows5, rows5, 128, 640, 128, y_pair[1]),
            (pl.ds(end, 1), pl.ds(end_to, 1), 512, 0, 128, next_pair[0]),
            (pl.ds(end, 1), pl.ds(end_to, 1), 128, 640, 128, next_pair[1]),
        )
        return [
            remote(
                cells.at[rf, half, pl.ds(lf, n)], cells.at[rt, half, pl.ds(lt, n)],
                ext_s.at[j, i], ext_r.at[j, i], device,
            )
            for i, (rf, rt, lf, lt, n, device) in enumerate(spots)
        ]

    ext = [edges(0), edges(1)]
    own_cells.wait()
    near.wait_recv()
    for c in ext[0]:
        c.start()
    for c in early:
        c.wait_recv()
    for c in ext[1]:
        c.start()
    w1_far.wait_recv()
    w1_on.start()
    w2_far[1].start()
    for c in late:
        c.wait_recv()
    w2_far[0].start()
    w2_near.start()
    own_bias.wait()
    for c in own_w:
        c.wait()
    for c in b_copies + [w1_near] + ext[0][1:3] + ext[1][1:3] + [w1_on]:
        c.wait_recv()

    def conv(source, l, x, dxs):
        stacked = jnp.concatenate(
            [
                jnp.concatenate([weights[l, dx * 9 + (dy * 3 + dz)] for dx in dxs for dy in range(3)], axis=1)
                for dz in range(3)
            ],
            axis=0,
        )
        totals = []
        for y in (0, 2):
            right = jnp.concatenate(
                [source[x + dx, :, (y + dy) * 128 : (y + dy + 2) * 128] for dx in dxs for dy in range(3)], axis=0
            )
            terms = jnp.dot(stacked, right, preferred_element_type=F32)
            for j in range(2):
                t = terms[:, j * 128 : (j + 1) * 128]
                totals.append(pltpu.roll(t[0:128], 1, axis=1) + t[128:256] + pltpu.roll(t[256:384], 127, axis=1))
        return totals

    def finish(total, l):
        return jnp.maximum(total + bias[:, l * 64 : l * 64 + 1], 0.0).astype(BF16)

    def line(t, side=None):
        q = xs if side is None else side
        return t + q * (3 - 2 * t)

    def first(t):
        x = line(t)
        for y, total in enumerate(conv(cells, 0, x, (0, 1, 2))):
            hidden[x + 1, :, (y + 1) * 128 : (y + 2) * 128] = finish(total, 0)

    def halo(i, x, to_x, device):
        return remote(
            hidden.at[pl.ds(x, 1), :, pl.ds(128, 512)], hidden.at[pl.ds(to_x, 1), :, pl.ds(128, 512)],
            h_s.at[i], h_r.at[i], device,
        )

    def columns(i, x, to_x, devices):
        return [
            remote(
                hidden.at[pl.ds(x, 1), :, pl.ds(lf, 128)], hidden.at[pl.ds(to_x, 1), :, pl.ds(lt, 128)],
                h_s.at[i + j], h_r.at[i + j], device,
            )
            for j, (lf, lt, device) in enumerate(((512, 0, devices[0]), (128, 640, devices[1])))
        ]

    to_mate = [halo(0, 1 + line(3), 5 * xs, mates[0])] + columns(1, 1 + line(3), 5 * xs, mate_pair)
    to_next = [halo(3, 1 + line(0), 5 * (1 - xs), x_next)] + columns(4, 1 + line(0), 5 * (1 - xs), next_pair)
    side = [columns(6 + 2 * t, 1 + line(t), 1 + line(t), y_pair) for t in range(4)]

    for j in (0, 1):
        for i in (0, 3, 4):
            ext[j][i].wait_recv()
    first(0)
    for c in to_next + side[0]:
        c.start()
    first(3)
    for c in to_mate + side[3]:
        c.start()
    first(1)
    for c in side[1]:
        c.start()
    for c in w2_far:
        c.wait_recv()
    w2_on.start()
    first(2)
    for c in side[2]:
        c.start()

    def spread(t, i):
        other = 2 * ((a + MATES[i][0]) % 2) + (k + MATES[i][1]) % 2
        return remote(
            result.at[pl.ds(line(t), 1), pl.ds(mo(32 * other, 32), 32), :],
            final.at[pl.ds(4 * xs + line(t), 1), :, pl.ds(mo(512 * ys, 512), 512)],
            o_s.at[i, t], o_r.at[i, t], mates[i],
        )

    def own_result(t):
        return pltpu.make_async_copy(
            result.at[pl.ds(line(t), 1), pl.ds(mine, 32), :],
            final.at[pl.ds(4 * xs + line(t), 1), :, pl.ds(mo(512 * ys, 512), 512)],
            own_sem.at[2 + t],
        )

    spreads = [[spread(t, i) for i in range(3)] for t in range(4)]
    own_results = [own_result(t) for t in range(4)]

    def second(t, totals):
        for y, total in enumerate(totals):
            result[line(t), :, y * 128 : (y + 1) * 128] = finish(total, 1)
        for c in spreads[t]:
            c.start()
        own_results[t].start()

    w2_near.wait_recv()
    w2_on.wait_recv()
    for t in (0, 3, 1, 2):
        for c in side[t]:
            c.wait_recv()
    second(1, conv(hidden, 1, line(1), (0, 1, 2)))
    second(2, conv(hidden, 1, line(2), (0, 1, 2)))
    for c in to_next:
        c.wait_recv()
    second(0, conv(hidden, 1, line(0), (0, 1, 2)))
    for c in to_mate:
        c.wait_recv()
    second(3, conv(hidden, 1, line(3), (0, 1, 2)))

    for t in (1, 2, 0, 3):
        own_results[t].wait()
        for c in spreads[t]:
            c.wait_recv()
        for x in (4 * xs + line(t), 4 * (1 - xs) + line(t, 1 - xs)):
            rows = jnp.stack([final[x, :, y * 128 : (y + 1) * 128] for y in range(8)], axis=0)
            out[:, pl.ds(x, 1)] = jnp.swapaxes(rows, 0, 1)[:, None]

    sent = early + late + [near] + b_copies + [w1_far, w1_near, w1_on, w2_near, w2_on] + w2_far
    sent += ext[0] + ext[1] + to_mate + to_next
    for t in range(4):
        sent += side[t] + spreads[t]
    for c in sent:
        c.wait_send()


def local(volume, weight_one, bias_one, weight_two, bias_two):
    vmem = pl.BlockSpec(memory_space=pltpu.VMEM)
    hbm = pl.BlockSpec(memory_space=pl.ANY)
    dma = pltpu.SemaphoreType.DMA
    out = pl.pallas_call(
        kernel,
        out_shape=pltpu.VMEM((32, 8, 8, 128), BF16),
        in_specs=[hbm] * 5,
        out_specs=vmem,
        scratch_shapes=[
            pltpu.VMEM((32, 8, 8, 128), BF16),
            pltpu.VMEM((1, 32), F32),
            pltpu.VMEM((1, 32), F32),
            pltpu.VMEM((8, 32, 1024), BF16),
            pltpu.VMEM((6, 128, 768), BF16),
            pltpu.VMEM((6, 128, 768), BF16),
            pltpu.VMEM((2, 27, 128, 128), BF16),
            pltpu.VMEM((32, 128), F32),
            pltpu.VMEM((128, 128), F32),
            pltpu.VMEM((4, 128, 512), BF16),
            pltpu.VMEM((8, 32, 1024), BF16),
            dma((5,)), dma((6,)),
            dma((3, 4)), dma((3, 4)),
            dma((2, 5)), dma((2, 5)),
            dma((7,)), dma((7,)),
            dma((3,)), dma((3,)),
            dma((14,)), dma((14,)),
            dma((3, 4)), dma((3, 4)),
        ],
        compiler_params=pltpu.CompilerParams(
            collective_id=0, has_side_effects=True, vmem_limit_bytes=60 * 2**20
        ),
        cost_estimate=pl.CostEstimate(flops=3_700_000_000, bytes_accessed=3_000_000, transcendentals=0),
    )(
        volume.reshape(32, 8, 8, 128),
        weight_one.reshape(27, 32, 128),
        weight_two.reshape(27, 32, 128),
        bias_one.reshape(1, 32),
        bias_two.reshape(1, 32),
    )
    return out.reshape(1, 32, 8, 8, 128)


def solution(mesh):
    in_specs = (
        P(None, "col", "gx", "gy", None),
        P(None, None, None, "col", None),
        P("col"),
        P(None, None, None, "col", None),
        P("col"),
    )
    out_specs = P(None, "col", "gx", "gy", None)
    return jax.shard_map(local, mesh=mesh, in_specs=in_specs, out_specs=out_specs, check_vma=False)
```

```python
import jax
import jax.numpy as jnp
from jax import lax
from jax.experimental import pallas as pl
from jax.experimental.pallas import tpu as pltpu
from jax.sharding import PartitionSpec as P

BF16 = jnp.bfloat16
F32 = jnp.float32
MESH = pl.DeviceIdType.MESH
MATES = ((1, 0), (1, 1), (0, 1))


def mo(value, unit):
    return pl.multiple_of(value, unit)


def kernel(
    vol_in, w1, w2, b1_in, b2_in, out,
    vol, b1, b2, part, cells, hidden, weights, bias_part, bias, result, final,
    in_sem, own_sem, mate_s, mate_r, ext_s, ext_r, w_s, w_r, b_s, b_r, h_s, h_r, o_s, o_r,
):
    gx, gy, col = lax.axis_index("gx"), lax.axis_index("gy"), lax.axis_index("col")
    a, k = col // 2, col % 2
    xs, ys = (a + gx + gy // 4) % 2, (k + gy) % 2
    big_x, big_y = 2 * gx + xs, 2 * gy + ys
    mine = mo(32 * col, 32)

    def at(to_x, to_y):
        to_x, to_y = (to_x + 16) % 16, (to_y + 16) % 16
        tx, ty = to_x // 2, to_y // 2
        return tx, ty, 2 * ((to_x % 2 + tx + ty // 4) % 2) + (to_y % 2 + ty) % 2

    mates = [(gx, gy, 2 * ((a + fx) % 2) + (k + fy) % 2) for fx, fy in MATES]
    sibling = mates[2]
    across = (gx, (gy + 4) % 8, 2 * (1 - a) + k)
    x_next = at(big_x + 2 * xs - 1, big_y)
    y_next = at(big_x, big_y + 2 * ys - 1)
    y_pair = at(big_x, big_y + 1), at(big_x, big_y - 1)
    next_pair = at(big_x + 2 * xs - 1, big_y + 1), at(big_x + 2 * xs - 1, big_y - 1)
    mate_pair = at(big_x + 1 - 2 * xs, big_y + 1), at(big_x + 1 - 2 * xs, big_y - 1)

    barrier = pltpu.get_barrier_semaphore()
    partners = mates + [across, x_next, y_next]
    for device in partners:
        pl.semaphore_signal(barrier, inc=1, device_id=device, device_id_type=MESH)

    def remote(src, dst, s, r, device):
        return pltpu.make_async_remote_copy(
            src_ref=src, dst_ref=dst, send_sem=s, recv_sem=r, device_id=device, device_id_type=MESH
        )

    fetch = [
        pltpu.make_async_copy(src, dst, in_sem.at[i])
        for i, (src, dst) in enumerate(((vol_in, vol), (b1_in, b1), (b2_in, b2)))
    ]
    own_w = [
        pltpu.make_async_copy(w, weights.at[l, :, pl.ds(mine, 32), :], in_sem.at[3 + l])
        for l, w in enumerate((w1, w2))
    ]
    for c in fetch + own_w:
        c.start()
    for c in fetch:
        c.wait()

    for x in range(8):
        rows = jnp.swapaxes(vol[:, x], 0, 1)
        for y in range(8):
            part[x, :, y * 128 : (y + 1) * 128] = rows[y]
    eye = lax.broadcasted_iota(jnp.int32, (32, 32), 0) == lax.broadcasted_iota(jnp.int32, (32, 32), 1)
    for l, b in enumerate((b1, b2)):
        column = jnp.sum(jnp.where(eye, b[...], 0.0), axis=1, keepdims=True)
        bias_part[:, l * 64 : (l + 1) * 64] = jnp.broadcast_to(column, (32, 64))

    pl.semaphore_wait(barrier, len(partners))

    def piece(x0, nx, y0, ny, to_x, to_y):
        return (
            part.at[pl.ds(x0, nx), :, pl.ds(mo(128 * y0, 128), 128 * ny)],
            cells.at[pl.ds(to_x, nx), pl.ds(mine, 32), pl.ds(128 * to_y, 128 * ny)],
        )

    early, late = [], []
    for i in range(2):
        xq, yq = (xs + MATES[i][0]) % 2, (ys + MATES[i][1]) % 2
        pieces = (
            piece(7 * xq, 1, 4 * yq, 4, 1 + 3 * xq, 1),
            piece(1 + 2 * xq, 4, 4 * yq, 1, 2 - 2 * xq, 1),
            piece(1 + 2 * xq, 4, 4 * yq + 3, 1, 2 - 2 * xq, 4),
            piece(1 + 2 * xq, 4, 4 * yq + 1, 2, 2 - 2 * xq, 2),
        )
        copies = [remote(s, d, mate_s.at[i, j], mate_r.at[i, j], mates[i]) for j, (s, d) in enumerate(pieces)]
        early.extend(copies[:3])
        late.append(copies[3])
    src, dst = piece(3 * xs, 5, 4 * ((ys + 1) % 2), 4, 1 - xs, 1)
    near = remote(src, dst, mate_s.at[2, 0], mate_r.at[2, 0], sibling)
    src, dst = piece(3 * xs, 5, 4 * ys, 4, 1 - xs, 1)
    own_cells = pltpu.make_async_copy(src, dst, own_sem.at[0])
    own_bias = pltpu.make_async_copy(bias_part, bias.at[pl.ds(mine, 32), :], own_sem.at[1])
    theirs = mo(64 * (1 - a) + 32 * k, 32)

    def send_w(l, w, first_tap, n_taps, i, device):
        slot = weights.at[l, pl.ds(first_tap, n_taps), pl.ds(mine, 32), :]
        return remote(w.at[pl.ds(first_tap, n_taps)], slot, w_s.at[i], w_r.at[i], device)

    def pass_w(l, i):
        slot = weights.at[l, :, pl.ds(theirs, 32), :]
        return remote(slot, slot, w_s.at[i], w_r.at[i], sibling)

    w1_far, w1_near, w1_on = send_w(0, w1, 0, 27, 0, across), send_w(0, w1, 0, 27, 1, sibling), pass_w(0, 2)
    w2_far = [send_w(1, w2, 0, 14, 3, mates[0]), send_w(1, w2, 14, 13, 4, across)]
    w2_near, w2_on = send_w(1, w2, 0, 27, 5, sibling), pass_w(1, 6)
    b_copies = [
        remote(bias_part, bias.at[pl.ds(mine, 32), :], b_s.at[i], b_r.at[i], mates[i]) for i in range(3)
    ]

    own_cells.start()
    near.start()
    for c in early:
        c.start()
    w1_far.start()
    w1_near.start()
    own_bias.start()
    for c in late:
        c.start()
    for c in b_copies:
        c.start()

    end, end_to = 1 + 3 * xs, 5 * (1 - xs)
    rows5 = pl.ds(1 - xs, 5)

    def edges(j):
        half = pl.ds(mo(64 * (a if j == 0 else 1 - a), 64), 64)
        spots = (
            (pl.ds(end, 1), pl.ds(end_to, 1), 128, 128, 512, x_next),
            (rows5, rows5, 512, 0, 128, y_pair[0]),
            (rows5, rows5, 128, 640, 128, y_pair[1]),
        )
        return [
            remote(
                cells.at[rf, half, pl.ds(lf, n)], cells.at[rt, half, pl.ds(lt, n)],
                ext_s.at[j, i], ext_r.at[j, i], device,
            )
            for i, (rf, rt, lf, lt, n, device) in enumerate(spots)
        ]

    ext = [edges(0), edges(1)]
    corners = [
        remote(
            cells.at[pl.ds(end, 1), :, pl.ds(lf, 128)], cells.at[pl.ds(end_to, 1), :, pl.ds(lt, 128)],
            ext_s.at[2, i], ext_r.at[2, i], device,
        )
        for i, (lf, lt, device) in enumerate(((512, 0, next_pair[0]), (128, 640, next_pair[1])))
    ]
    own_cells.wait()
    near.wait_recv()
    for c in ext[0]:
        c.start()
    for c in early:
        c.wait_recv()
    for c in ext[1]:
        c.start()
    for c in ext[0][1:]:
        c.wait_recv()
    for c in corners:
        c.start()
    w1_far.wait_recv()
    w1_on.start()
    w2_far[1].start()
    for c in late:
        c.wait_recv()
    w2_far[0].start()
    w2_near.start()
    own_bias.wait()
    for c in own_w:
        c.wait()
    for c in b_copies + [w1_near, w1_on]:
        c.wait_recv()

    def finish(total, l):
        return jnp.maximum(total + bias[:, l * 64 : l * 64 + 1], 0.0).astype(BF16)

    def line(t, side=None):
        q = xs if side is None else side
        return t + q * (3 - 2 * t)

    def apply(left, right):
        terms = jnp.dot(left, right, preferred_element_type=F32)
        totals = []
        for j in range(2):
            t = terms[:, j * 128 : (j + 1) * 128]
            totals.append(pltpu.roll(t[0:128], 1, axis=1) + t[128:256] + pltpu.roll(t[256:384], 127, axis=1))
        return totals

    def stack(l, taps):
        return jnp.concatenate(
            [jnp.concatenate([weights[l, 3 * q + dz] for q in taps], axis=1) for dz in range(3)], axis=0
        )

    def gather(source, spots):
        return jnp.concatenate(
            [
                jnp.concatenate(
                    [source[line(t) + q // 3, :, (y + q % 3) * 128 : (y + q % 3 + 1) * 128] for t, y in spots], axis=1
                )
                for q in range(9)
            ],
            axis=0,
        )

    def first(*spots):
        for (t, y), total in zip(spots, apply(stack(0, range(9)), gather(cells, spots))):
            hidden[line(t) + 1, :, (y + 1) * 128 : (y + 2) * 128] = finish(total, 0)

    def halo(i, x, to_x, device):
        return remote(
            hidden.at[pl.ds(x, 1), :, pl.ds(128, 512)], hidden.at[pl.ds(to_x, 1), :, pl.ds(128, 512)],
            h_s.at[i], h_r.at[i], device,
        )

    def columns(i, x, to_x, devices, n=1):
        return [
            remote(
                hidden.at[pl.ds(x, n), :, pl.ds(lf, 128)], hidden.at[pl.ds(to_x, n), :, pl.ds(lt, 128)],
                h_s.at[i + j], h_r.at[i + j], device,
            )
            for j, (lf, lt, device) in enumerate(((512, 0, devices[0]), (128, 640, devices[1])))
        ]

    to_mate = [halo(0, 1 + line(3), 5 * xs, mates[0])] + columns(1, 1 + line(3), 5 * xs, mate_pair)
    to_next = [halo(3, 1 + line(0), 5 * (1 - xs), x_next)] + columns(4, 1 + line(0), 5 * (1 - xs), next_pair)
    side = {t: columns(6 + 2 * t, 1 + line(t), 1 + line(t), y_pair) for t in (0, 3)}
    side[1] = columns(8, 2, 2, y_pair, 2)

    first((3, 1), (3, 2))
    first((1, 1), (1, 2))
    first((2, 1), (2, 2))
    for c in ext[1] + [ext[0][0]] + corners:
        c.wait_recv()
    first((0, 0), (0, 1))
    first((0, 2), (0, 3))
    for c in to_next + side[0]:
        c.start()
    first((3, 0), (3, 3))
    for c in to_mate + side[3]:
        c.start()
    first((1, 0), (2, 0))
    first((1, 3), (2, 3))
    for c in side[1]:
        c.start()
    for c in w2_far:
        c.wait_recv()
    w2_on.start()

    def spread(x, n, i, slot):
        other = 2 * ((a + MATES[i][0]) % 2) + (k + MATES[i][1]) % 2
        return remote(
            result.at[pl.ds(x, n), pl.ds(mo(32 * other, 32), 32), :],
            final.at[pl.ds(4 * xs + x, n), :, pl.ds(mo(512 * ys, 512), 512)],
            o_s.at[i, slot], o_r.at[i, slot], mates[i],
        )

    def own_result(x, n, slot):
        return pltpu.make_async_copy(
            result.at[pl.ds(x, n), pl.ds(mine, 32), :],
            final.at[pl.ds(4 * xs + x, n), :, pl.ds(mo(512 * ys, 512), 512)],
            own_sem.at[2 + slot],
        )

    spans = {0: (line(0), 1), 1: (1, 2), 3: (line(3), 1)}
    spreads = {t: [spread(x, n, i, t) for i in range(3)] for t, (x, n) in spans.items()}
    own_results = {t: own_result(x, n, t) for t, (x, n) in spans.items()}

    def second(*spots):
        for (t, y), total in zip(spots, apply(stack(1, range(9)), gather(hidden, spots))):
            result[line(t), :, y * 128 : (y + 1) * 128] = finish(total, 1)

    def send_out(*lines):
        for t in lines:
            for c in spreads[t]:
                c.start()
            own_results[t].start()

    w2_near.wait_recv()
    w2_on.wait_recv()
    second((1, 1), (1, 2))
    second((2, 1), (2, 2))
    for t in (0, 3, 1):
        for c in side[t]:
            c.wait_recv()
    second((1, 0), (2, 0))
    second((1, 3), (2, 3))
    send_out(1)
    for c in to_next:
        c.wait_recv()
    second((0, 0), (0, 1))
    second((0, 2), (0, 3))
    send_out(0)
    for c in to_mate:
        c.wait_recv()
    second((3, 0), (3, 1))
    second((3, 2), (3, 3))
    send_out(3)

    for t in (1, 0, 3):
        own_results[t].wait()
        for c in spreads[t]:
            c.wait_recv()
        for x in (1, 2, 5, 6) if t == 1 else (4 * xs + line(t), 4 * (1 - xs) + line(t, 1 - xs)):
            rows = jnp.stack([final[x, :, y * 128 : (y + 1) * 128] for y in range(8)], axis=0)
            out[:, pl.ds(x, 1)] = jnp.swapaxes(rows, 0, 1)[:, None]

    sent = early + late + [near] + b_copies + [w1_far, w1_near, w1_on, w2_near, w2_on] + w2_far
    sent += ext[0] + ext[1] + corners + to_mate + to_next
    for t in (0, 1, 3):
        sent += side[t] + spreads[t]
    for c in sent:
        c.wait_send()


def local(volume, weight_one, bias_one, weight_two, bias_two):
    vmem = pl.BlockSpec(memory_space=pltpu.VMEM)
    hbm = pl.BlockSpec(memory_space=pl.ANY)
    dma = pltpu.SemaphoreType.DMA
    out = pl.pallas_call(
        kernel,
        out_shape=pltpu.VMEM((32, 8, 8, 128), BF16),
        in_specs=[hbm] * 5,
        out_specs=vmem,
        scratch_shapes=[
            pltpu.VMEM((32, 8, 8, 128), BF16),
            pltpu.VMEM((1, 32), F32),
            pltpu.VMEM((1, 32), F32),
            pltpu.VMEM((8, 32, 1024), BF16),
            pltpu.VMEM((6, 128, 768), BF16),
            pltpu.VMEM((6, 128, 768), BF16),
            pltpu.VMEM((2, 27, 128, 128), BF16),
            pltpu.VMEM((32, 128), F32),
            pltpu.VMEM((128, 128), F32),
            pltpu.VMEM((4, 128, 512), BF16),
            pltpu.VMEM((8, 32, 1024), BF16),
            dma((5,)), dma((6,)),
            dma((3, 4)), dma((3, 4)),
            dma((3, 3)), dma((3, 3)),
            dma((7,)), dma((7,)),
            dma((3,)), dma((3,)),
            dma((14,)), dma((14,)),
            dma((3, 4)), dma((3, 4)),
        ],
        compiler_params=pltpu.CompilerParams(
            collective_id=0, has_side_effects=True, vmem_limit_bytes=60 * 2**20
        ),
        cost_estimate=pl.CostEstimate(flops=3_700_000_000, bytes_accessed=3_000_000, transcendentals=0),
    )(
        volume.reshape(32, 8, 8, 128),
        weight_one.reshape(27, 32, 128),
        weight_two.reshape(27, 32, 128),
        bias_one.reshape(1, 32),
        bias_two.reshape(1, 32),
    )
    return out.reshape(1, 32, 8, 8, 128)


def solution(mesh):
    in_specs = (
        P(None, "col", "gx", "gy", None),
        P(None, None, None, "col", None),
        P("col"),
        P(None, None, None, "col", None),
        P("col"),
    )
    out_specs = P(None, "col", "gx", "gy", None)
    return jax.shard_map(local, mesh=mesh, in_specs=in_specs, out_specs=out_specs, check_vma=False)
```

```python
import jax
import jax.numpy as jnp
from jax import lax
from jax.experimental import pallas as pl
from jax.experimental.pallas import tpu as pltpu
from jax.sharding import PartitionSpec as P

BF16 = jnp.bfloat16
F32 = jnp.float32
MESH = pl.DeviceIdType.MESH
MATES = ((1, 0), (1, 1), (0, 1))


def mo(value, unit):
    return pl.multiple_of(value, unit)


def kernel(
    vol_in, w1, w2, b1_in, b2_in, out,
    vol, b1, b2, part, cells, hidden, weights, bias_part, bias, sums, result, final,
    in_sem, own_sem, mate_s, mate_r, ext_s, ext_r, w_s, w_r, b_s, b_r, h_s, h_r, o_s, o_r,
):
    gx, gy, col = lax.axis_index("gx"), lax.axis_index("gy"), lax.axis_index("col")
    a, k = col // 2, col % 2
    xs, ys = (a + gx + gy // 4) % 2, (k + gy) % 2
    big_x, big_y = 2 * gx + xs, 2 * gy + ys
    mine = mo(32 * col, 32)

    def at(to_x, to_y):
        to_x, to_y = (to_x + 16) % 16, (to_y + 16) % 16
        tx, ty = to_x // 2, to_y // 2
        return tx, ty, 2 * ((to_x % 2 + tx + ty // 4) % 2) + (to_y % 2 + ty) % 2

    mates = [(gx, gy, 2 * ((a + fx) % 2) + (k + fy) % 2) for fx, fy in MATES]
    sibling = mates[2]
    across = (gx, (gy + 4) % 8, 2 * (1 - a) + k)
    x_next = at(big_x + 2 * xs - 1, big_y)
    y_next = at(big_x, big_y + 2 * ys - 1)
    y_pair = at(big_x, big_y + 1), at(big_x, big_y - 1)
    next_pair = at(big_x + 2 * xs - 1, big_y + 1), at(big_x + 2 * xs - 1, big_y - 1)
    mate_pair = at(big_x + 1 - 2 * xs, big_y + 1), at(big_x + 1 - 2 * xs, big_y - 1)

    barrier = pltpu.get_barrier_semaphore()
    partners = mates + [across, x_next, y_next]
    for device in partners:
        pl.semaphore_signal(barrier, inc=1, device_id=device, device_id_type=MESH)

    def remote(src, dst, s, r, device):
        return pltpu.make_async_remote_copy(
            src_ref=src, dst_ref=dst, send_sem=s, recv_sem=r, device_id=device, device_id_type=MESH
        )

    fetch = [
        pltpu.make_async_copy(src, dst, in_sem.at[i])
        for i, (src, dst) in enumerate(((vol_in, vol), (b1_in, b1), (b2_in, b2)))
    ]
    own_w = [
        pltpu.make_async_copy(w, weights.at[l, :, pl.ds(mine, 32), :], in_sem.at[3 + l])
        for l, w in enumerate((w1, w2))
    ]
    for c in fetch + own_w:
        c.start()
    for c in fetch:
        c.wait()

    for x in range(8):
        part[x] = jnp.swapaxes(vol[:, x], 0, 1)
    eye = lax.broadcasted_iota(jnp.int32, (32, 32), 0) == lax.broadcasted_iota(jnp.int32, (32, 32), 1)
    for l, b in enumerate((b1, b2)):
        column = jnp.sum(jnp.where(eye, b[...], 0.0), axis=1, keepdims=True)
        bias_part[:, l * 64 : (l + 1) * 64] = jnp.broadcast_to(column, (32, 64))

    pl.semaphore_wait(barrier, len(partners))

    def piece(x0, nx, y0, ny, to_x, to_y):
        return (
            part.at[pl.ds(x0, nx), pl.ds(y0, ny)],
            cells.at[pl.ds(to_x, nx), pl.ds(to_y, ny), pl.ds(mine, 32)],
        )

    early, late = [], []
    for i in range(2):
        xq, yq = (xs + MATES[i][0]) % 2, (ys + MATES[i][1]) % 2
        pieces = (
            piece(7 * xq, 1, 4 * yq, 4, 1 + 3 * xq, 1),
            piece(1 + 2 * xq, 4, 4 * yq, 1, 2 - 2 * xq, 1),
            piece(1 + 2 * xq, 4, 4 * yq + 3, 1, 2 - 2 * xq, 4),
            piece(1 + 2 * xq, 4, 4 * yq + 1, 2, 2 - 2 * xq, 2),
        )
        copies = [remote(s, d, mate_s.at[i, j], mate_r.at[i, j], mates[i]) for j, (s, d) in enumerate(pieces)]
        early.extend(copies[:3])
        late.append(copies[3])
    src, dst = piece(3 * xs, 5, 4 * ((ys + 1) % 2), 4, 1 - xs, 1)
    near = remote(src, dst, mate_s.at[2, 0], mate_r.at[2, 0], sibling)
    src, dst = piece(3 * xs, 5, 4 * ys, 4, 1 - xs, 1)
    own_cells = pltpu.make_async_copy(src, dst, own_sem.at[0])
    own_bias = pltpu.make_async_copy(bias_part, bias.at[pl.ds(mine, 32), :], own_sem.at[1])
    theirs = mo(64 * (1 - a) + 32 * k, 32)

    def send_w(l, w, first_tap, n_taps, i, device):
        slot = weights.at[l, pl.ds(first_tap, n_taps), pl.ds(mine, 32), :]
        return remote(w.at[pl.ds(first_tap, n_taps)], slot, w_s.at[i], w_r.at[i], device)

    def pass_w(l, i):
        slot = weights.at[l, :, pl.ds(theirs, 32), :]
        return remote(slot, slot, w_s.at[i], w_r.at[i], sibling)

    w1_far, w1_near, w1_on = send_w(0, w1, 0, 27, 0, across), send_w(0, w1, 0, 27, 1, sibling), pass_w(0, 2)
    w2_far = [send_w(1, w2, 0, 14, 3, mates[0]), send_w(1, w2, 14, 13, 4, across)]
    w2_near, w2_on = send_w(1, w2, 0, 27, 5, sibling), pass_w(1, 6)
    b_copies = [
        remote(bias_part, bias.at[pl.ds(mine, 32), :], b_s.at[i], b_r.at[i], mates[i]) for i in range(3)
    ]

    own_cells.start()
    near.start()
    for c in early:
        c.start()
    w1_far.start()
    w1_near.start()
    own_bias.start()
    for c in late:
        c.start()
    for c in b_copies:
        c.start()

    end, end_to = 1 + 3 * xs, 5 * (1 - xs)
    rows5 = pl.ds(1 - xs, 5)

    def edges(j):
        half = pl.ds(mo(64 * (a if j == 0 else 1 - a), 64), 64)
        spots = (
            (pl.ds(end, 1), pl.ds(end_to, 1), 1, 1, 4, x_next),
            (rows5, rows5, 4, 0, 1, y_pair[0]),
            (rows5, rows5, 1, 5, 1, y_pair[1]),
        )
        return [
            remote(
                cells.at[rf, pl.ds(cf, n), half], cells.at[rt, pl.ds(ct, n), half],
                ext_s.at[j, i], ext_r.at[j, i], device,
            )
            for i, (rf, rt, cf, ct, n, device) in enumerate(spots)
        ]

    ext = [edges(0), edges(1)]
    corners = [
        remote(
            cells.at[pl.ds(end, 1), pl.ds(cf, 1)], cells.at[pl.ds(end_to, 1), pl.ds(ct, 1)],
            ext_s.at[2, i], ext_r.at[2, i], device,
        )
        for i, (cf, ct, device) in enumerate(((4, 0, next_pair[0]), (1, 5, next_pair[1])))
    ]
    own_cells.wait()
    near.wait_recv()
    for c in ext[0]:
        c.start()
    for c in early:
        c.wait_recv()
    for c in ext[1]:
        c.start()
    for c in ext[0][1:]:
        c.wait_recv()
    for c in corners:
        c.start()
    w1_far.wait_recv()
    w1_on.start()
    w2_far[1].start()
    for c in late:
        c.wait_recv()
    w2_far[0].start()
    w2_near.start()
    own_bias.wait()
    for c in own_w:
        c.wait()
    for c in b_copies + [w1_near, w1_on]:
        c.wait_recv()

    def finish(total, l):
        return jnp.maximum(total + bias[:, l * 64 : l * 64 + 1], 0.0).astype(BF16)

    def line(t, side=None):
        q = xs if side is None else side
        return t + q * (3 - 2 * t)

    def apply(left, right):
        terms = jnp.dot(left, right, preferred_element_type=F32)
        totals = []
        for j in range(2):
            t = terms[:, j * 128 : (j + 1) * 128]
            totals.append(pltpu.roll(t[0:128], 1, axis=1) + t[128:256] + pltpu.roll(t[256:384], 127, axis=1))
        return totals

    def stack(l, taps):
        return jnp.concatenate(
            [jnp.concatenate([weights[l, 3 * q + dz] for q in taps], axis=1) for dz in range(3)], axis=0
        )

    def gather(source, spots):
        return jnp.concatenate(
            [
                jnp.concatenate(
                    [source[line(t) + q // 3, y + q % 3] for t, y in spots], axis=1
                )
                for q in range(9)
            ],
            axis=0,
        )

    def first(*spots):
        for (t, y), total in zip(spots, apply(stack(0, range(9)), gather(cells, spots))):
            hidden[line(t) + 1, y + 1] = finish(total, 0)

    def halo(i, x, to_x, device):
        return remote(
            hidden.at[pl.ds(x, 1), pl.ds(1, 4)], hidden.at[pl.ds(to_x, 1), pl.ds(1, 4)],
            h_s.at[i], h_r.at[i], device,
        )

    def columns(i, x, to_x, devices, n=1):
        return [
            remote(
                hidden.at[pl.ds(x, n), pl.ds(cf, 1)], hidden.at[pl.ds(to_x, n), pl.ds(ct, 1)],
                h_s.at[i + j], h_r.at[i + j], device,
            )
            for j, (cf, ct, device) in enumerate(((4, 0, devices[0]), (1, 5, devices[1])))
        ]

    to_mate = [halo(0, 1 + line(3), 5 * xs, mates[0])] + columns(1, 1 + line(3), 5 * xs, mate_pair)
    to_next = [halo(3, 1 + line(0), 5 * (1 - xs), x_next)] + columns(4, 1 + line(0), 5 * (1 - xs), next_pair)
    side = {t: columns(6 + 2 * t, 1 + line(t), 1 + line(t), y_pair) for t in (0, 3)}
    side[1] = columns(8, 2, 2, y_pair, 2)

    first((3, 1), (3, 2))
    first((1, 1), (1, 2))
    first((2, 1), (2, 2))
    for c in ext[1] + [ext[0][0]] + corners:
        c.wait_recv()
    first((0, 0), (0, 1))
    first((0, 2), (0, 3))
    for c in to_next + side[0]:
        c.start()
    first((3, 0), (3, 3))
    for c in to_mate + side[3]:
        c.start()
    first((1, 0), (2, 0))
    first((1, 3), (2, 3))
    for c in side[1]:
        c.start()
    for c in w2_far:
        c.wait_recv()
    w2_on.start()

    def spread(x, n, i, slot):
        other = 2 * ((a + MATES[i][0]) % 2) + (k + MATES[i][1]) % 2
        return remote(
            result.at[pl.ds(x, n), :, pl.ds(mo(32 * other, 32), 32)],
            final.at[pl.ds(4 * xs + x, n), pl.ds(4 * ys, 4)],
            o_s.at[i, slot], o_r.at[i, slot], mates[i],
        )

    def own_result(x, n, slot):
        return pltpu.make_async_copy(
            result.at[pl.ds(x, n), :, pl.ds(mine, 32)],
            final.at[pl.ds(4 * xs + x, n), pl.ds(4 * ys, 4)],
            own_sem.at[2 + slot],
        )

    spans = {0: (line(0), 1), 1: (1, 2), 3: (line(3), 1)}
    spreads = {t: [spread(x, n, i, t) for i in range(3)] for t, (x, n) in spans.items()}
    own_results = {t: own_result(x, n, t) for t, (x, n) in spans.items()}

    def second(*spots):
        for (t, y), total in zip(spots, apply(stack(1, range(9)), gather(hidden, spots))):
            result[line(t), y] = finish(total, 1)

    def part_of(t, spots, dxs):
        taps = [(dx, dy) for dx in dxs for dy in range(3)]
        left = jnp.concatenate(
            [jnp.concatenate([weights[1, dx * 9 + (3 * dy + dz)] for dx, dy in taps], axis=1) for dz in range(3)],
            axis=0,
        )
        right = jnp.concatenate(
            [jnp.concatenate([hidden[line(t) + dx, y + dy] for y in spots], axis=1) for dx, dy in taps], axis=0
        )
        return zip(spots, apply(left, right))

    def begin(t, *spots):
        for y, total in part_of(t, spots, (1 - xs, 2 - xs) if t == 0 else (xs, 1 + xs)):
            sums[t // 3, y] = total

    def close(t, *spots):
        for y, total in part_of(t, spots, (2 * xs,) if t == 0 else (2 - 2 * xs,)):
            result[line(t), y] = finish(total + sums[t // 3, y], 1)

    def send_out(*lines):
        for t in lines:
            for c in spreads[t]:
                c.start()
            own_results[t].start()

    w2_near.wait_recv()
    w2_on.wait_recv()
    second((1, 1), (1, 2))
    second((2, 1), (2, 2))
    begin(0, 1, 2)
    begin(3, 1, 2)
    for t in (0, 3, 1):
        for c in side[t]:
            c.wait_recv()
    second((1, 0), (2, 0))
    second((1, 3), (2, 3))
    send_out(1)
    begin(0, 0, 3)
    begin(3, 0, 3)
    for c in to_next:
        c.wait_recv()
    close(0, 1, 2)
    close(0, 0, 3)
    send_out(0)
    for c in to_mate:
        c.wait_recv()
    close(3, 1, 2)
    close(3, 0, 3)
    send_out(3)

    for t in (1, 0, 3):
        own_results[t].wait()
        for c in spreads[t]:
            c.wait_recv()
        for x in (1, 2, 5, 6) if t == 1 else (4 * xs + line(t), 4 * (1 - xs) + line(t, 1 - xs)):
            out[:, pl.ds(x, 1)] = jnp.swapaxes(final[x], 0, 1)[:, None]

    sent = early + late + [near] + b_copies + [w1_far, w1_near, w1_on, w2_near, w2_on] + w2_far
    sent += ext[0] + ext[1] + corners + to_mate + to_next
    for t in (0, 1, 3):
        sent += side[t] + spreads[t]
    for c in sent:
        c.wait_send()


def local(volume, weight_one, bias_one, weight_two, bias_two):
    vmem = pl.BlockSpec(memory_space=pltpu.VMEM)
    hbm = pl.BlockSpec(memory_space=pl.ANY)
    dma = pltpu.SemaphoreType.DMA
    out = pl.pallas_call(
        kernel,
        out_shape=pltpu.VMEM((32, 8, 8, 128), BF16),
        in_specs=[hbm] * 5,
        out_specs=vmem,
        scratch_shapes=[
            pltpu.VMEM((32, 8, 8, 128), BF16),
            pltpu.VMEM((1, 32), F32),
            pltpu.VMEM((1, 32), F32),
            pltpu.VMEM((8, 8, 32, 128), BF16),
            pltpu.VMEM((6, 6, 128, 128), BF16),
            pltpu.VMEM((6, 6, 128, 128), BF16),
            pltpu.VMEM((2, 27, 128, 128), BF16),
            pltpu.VMEM((32, 128), F32),
            pltpu.VMEM((128, 128), F32),
            pltpu.VMEM((2, 4, 128, 128), F32),
            pltpu.VMEM((4, 4, 128, 128), BF16),
            pltpu.VMEM((8, 8, 32, 128), BF16),
            dma((5,)), dma((6,)),
            dma((3, 4)), dma((3, 4)),
            dma((3, 3)), dma((3, 3)),
            dma((7,)), dma((7,)),
            dma((3,)), dma((3,)),
            dma((14,)), dma((14,)),
            dma((3, 4)), dma((3, 4)),
        ],
        compiler_params=pltpu.CompilerParams(
            collective_id=0, has_side_effects=True, vmem_limit_bytes=60 * 2**20
        ),
        cost_estimate=pl.CostEstimate(flops=3_700_000_000, bytes_accessed=3_000_000, transcendentals=0),
    )(
        volume.reshape(32, 8, 8, 128),
        weight_one.reshape(27, 32, 128),
        weight_two.reshape(27, 32, 128),
        bias_one.reshape(1, 32),
        bias_two.reshape(1, 32),
    )
    return out.reshape(1, 32, 8, 8, 128)


def solution(mesh):
    in_specs = (
        P(None, "col", "gx", "gy", None),
        P(None, None, None, "col", None),
        P("col"),
        P(None, None, None, "col", None),
        P("col"),
    )
    out_specs = P(None, "col", "gx", "gy", None)
    return jax.shard_map(local, mesh=mesh, in_specs=in_specs, out_specs=out_specs, check_vma=False)
```
